256 devices in a mesh: chan: 16 (over x, y_lo, core), win: 16 (over y_hi, z).
Axes of the slice: x: 4, y: 4 (y_hi: 2, y_lo: 2; y = y_hi * 2 + y_lo), z: 8, core: 2. Of those that a mesh axis runs over, the one named last changes fastest.
Arguments:
- strain: bfloat16 [4096, 16384], P('chan', 'win'), may hold values from -6 to 6
- alive_flags: int32 [4096], P('chan'), may hold values 0 or 1
Outputs:
- correlation: float32 [4096, 2, 4096], P('win', None, 'chan')
The draws below stay inside these ranges and needn't reach their ends.
All inputs are finite; a program needn't handle non-finite values. No bound on the sum of `alive_flags` on one device may be relied on, other than what follows from the above.
Results may differ from the reference program's by a relative error of at most 0.0059.
Values may be sent and summed in bfloat16 or wider, within the bound.
A program may use at most 128 MiB of HBM per device.

```python
import math
import jax
import jax.numpy as jnp
from jax import lax

CHANNELS = 4096
NF = 256
FIRST_BIN = 64
SEG = 1024
TREND_REACH = 8
LEVEL_REACH = 32
BIN_REACH = 4
LAGS = 2
SEGMENTS = 16
TIME = 16384
N_CHAN = 16


def touch_ends(result, stream_key, smallest, high):
    index_at = [jax.random.randint(jax.random.fold_in(stream_key, axis), (), 0, length) for axis, length in enumerate(result.shape)]
    longest = result.shape.index(max(result.shape))
    neighbour = index_at[:longest] + [(index_at[longest] + 1) % result.shape[longest]] + index_at[longest + 1:]
    return result.at[tuple(index_at)].set(smallest).at[tuple(neighbour)].set(high)


def levels(key, shape, shards, smallest, largest):
    def one(axis_at, parts):
        heights = jax.random.uniform(jax.random.fold_in(jax.random.fold_in(key, 6), axis_at), (parts,), jnp.float32, smallest / len(shards), largest / len(shards))
        return jnp.repeat(jnp.exp(heights), shape[axis_at] // parts).reshape((-1,) + (1,) * (len(shape) - axis_at - 1))

    factor_of = one(*shards[0])
    for cut in shards[1:]:
        factor_of = factor_of * one(*cut)
    return factor_of


def gaussian(rng, shape, scale, bound, split=(), kind=jnp.bfloat16):
    level = levels(rng, shape, split, -0.22, 0.18) if split else 1.0
    entries = jax.random.normal(rng, shape, jnp.float32) * scale * level
    return jnp.minimum(jnp.maximum(entries, -bound), bound).astype(kind)


def setup_inputs(seed: int = 0) -> dict:
    arg_keys = jax.random.split(jax.random.key(seed), 3)
    strain = gaussian(arg_keys[0], (CHANNELS, TIME), 1.0, 6.0, ((0, 16), (1, 16)))
    alive_flags = touch_ends((jax.random.randint(arg_keys[1], (CHANNELS,), 0, 8) < 7).astype(jnp.int32), jax.random.fold_in(arg_keys[1], 1), 0, 1)
    return {"strain": strain, "alive_flags": alive_flags}


def window_sum(values, window_len):
    window_dims = (1,) * (values.ndim - 1) + (window_len,)
    return lax.reduce_window(values, jnp.zeros((), values.dtype), lax.add, window_dims, (1,) * values.ndim, 'VALID')

def condition(padded, trend_reach, level_reach):
    padded_len = padded.shape[-1]
    trend_mean = window_sum(padded, 2 * trend_reach + 1) / (2 * trend_reach + 1)
    detrended = padded[:, trend_reach:padded_len - trend_reach] - trend_mean
    inner_len = detrended.shape[-1]
    level_mean = window_sum(jnp.abs(detrended), 2 * level_reach + 1) / (2 * level_reach + 1)
    return detrended[:, level_reach:inner_len - level_reach] / (level_mean + 1e-05)

def dft_table(seg_len, bin_count, first_bin):
    sample_idx = jnp.arange(seg_len, dtype=jnp.int32)[:, None]
    bin_idx = jnp.arange(bin_count, dtype=jnp.int32)[None, :] + first_bin
    phase_angle = 2.0 * math.pi / seg_len * (sample_idx * bin_idx % seg_len).astype(jnp.float32)
    return jnp.concatenate([jnp.cos(phase_angle), -jnp.sin(phase_angle)], axis=1).astype(jnp.bfloat16)

def lag_tables(seg_len, bin_count, first_bin, lag_count):
    lag_idx = jnp.arange(lag_count, dtype=jnp.int32)[:, None]
    lag_shift = 2 * (2 * lag_idx - lag_count + 1)
    bin_idx = jnp.arange(bin_count, dtype=jnp.int32)[None, :] + first_bin
    phase_angle = 2.0 * math.pi / seg_len * (bin_idx * lag_shift % seg_len).astype(jnp.float32)
    return (jnp.cos(phase_angle), jnp.sin(phase_angle))

def whiten(spectra, alive_col, bin_count, bin_reach):
    real_part = spectra[..., :bin_count]
    imag_part = spectra[..., bin_count:]
    magnitude = jnp.sqrt(real_part * real_part + imag_part * imag_part)
    pad_spec = ((0, 0),) * (magnitude.ndim - 1) + ((bin_reach, bin_reach),)
    smoothed = window_sum(jnp.pad(magnitude, pad_spec), 2 * bin_reach + 1) / (2 * bin_reach + 1)
    level_mean = lax.optimization_barrier(jnp.mean(magnitude, axis=-1, keepdims=True))
    factor = alive_col / (smoothed + level_mean + 1e-05)
    return jnp.concatenate([real_part * factor, imag_part * factor], axis=-1).astype(jnp.bfloat16)

def rotate(panel, lag_cos, lag_sin, bin_count):
    row_count = panel.shape[0]
    split_parts = panel.astype(jnp.float32).reshape(row_count, -1, 2, bin_count)
    real_part = split_parts[None, :, :, 0, :]
    imag_part = split_parts[None, :, :, 1, :]
    cosine = lag_cos[:, None, None, :]
    sine_part = lag_sin[:, None, None, :]
    turned = jnp.stack([real_part * cosine + imag_part * sine_part, imag_part * cosine - real_part * sine_part], axis=3)
    return turned.reshape(lag_cos.shape[0], row_count, -1).astype(jnp.bfloat16)

def reference(strain, alive_flags):
    margin = TREND_REACH + LEVEL_REACH
    row_count = CHANNELS // N_CHAN
    table = dft_table(SEG, NF, FIRST_BIN).astype(jnp.float32)
    blocks = strain.reshape(N_CHAN, row_count, SEG * SEGMENTS)
    flags = alive_flags.reshape(N_CHAN, row_count)

    def spectra_of(block_item):
        chan_block, chan_flags = block_item
        padded = jnp.pad(chan_block.astype(jnp.float32), ((0, 0), (margin, margin)))
        normal = condition(padded, TREND_REACH, LEVEL_REACH)
        pieces = lax.optimization_barrier(normal.astype(jnp.bfloat16)).astype(jnp.float32)
        spectra = jnp.dot(pieces.reshape(row_count * SEGMENTS, SEG), table, precision=lax.Precision.HIGHEST)
        spectra = spectra.reshape(row_count, SEGMENTS, 2 * NF)
        white = whiten(spectra, chan_flags.astype(jnp.float32)[:, None, None], NF, BIN_REACH)
        return white.reshape(row_count, SEGMENTS * 2 * NF)
    white = lax.map(spectra_of, (blocks, flags)).reshape(CHANNELS, SEGMENTS * 2 * NF)
    white = lax.optimization_barrier(white)
    lag_cos, lag_sin = lag_tables(SEG, NF, FIRST_BIN, LAGS)
    turned = lax.optimization_barrier(rotate(white, lag_cos, lag_sin, NF))
    own_spectra = white.astype(jnp.float32)

    def one_lag(turned_panel):
        return jnp.dot(turned_panel.astype(jnp.float32), own_spectra.T, precision=lax.Precision.HIGHEST)
    lag_planes = lax.map(one_lag, turned)
    stack_scale = 1.0 / math.sqrt(NF * SEGMENTS)
    return jnp.transpose(lag_planes, (1, 0, 2)) * stack_scale
```

```python
import functools
import math

import jax
import jax.numpy as jnp
import ml_dtypes
import numpy as np
from jax import lax
from jax.experimental import pallas as pl
from jax.experimental.pallas import tpu as pltpu
from jax.sharding import PartitionSpec as P

NF = 256
FIRST_BIN = 64
SEG = 1024
TREND_REACH = 8
LEVEL_REACH = 32
BIN_REACH = 4
LAGS = 2
MESH = pl.DeviceIdType.MESH

TREND = 2 * TREND_REACH + 1
LEVEL = 2 * LEVEL_REACH + 1
SMOOTH = 2 * BIN_REACH + 1
STEPS = 8
DEEPEST = 3


def constants():
    bf16 = ml_dtypes.bfloat16
    off = np.arange(512)[:, None] - 128 - np.arange(256)[None, :]
    trend = TREND * (off == 0) - 1.0 * (np.abs(off) <= TREND_REACH)
    level = 1.0 * (np.abs(off) <= LEVEL_REACH)
    k = np.arange(SEG)[:, None]
    f = np.arange(NF)[None, :] + FIRST_BIN
    angle = 2.0 * math.pi / SEG * (k * f % SEG)
    table = np.concatenate([np.cos(angle), -np.sin(angle)], axis=1)
    bins = np.arange(NF)
    near = 1.0 * (np.abs(bins[:, None] - bins[None, :]) <= BIN_REACH)
    smooth = np.concatenate([near, np.ones((NF, NF))], axis=1)
    theta = 2.0 * math.pi / SEG * (f * 2 % SEG)
    turn = np.concatenate([np.cos(theta), np.sin(theta)], axis=0)
    turn = np.concatenate([turn, np.zeros((6, NF))], axis=0)
    return (
        trend.astype(bf16),
        level.astype(bf16),
        table.astype(bf16),
        smooth.astype(bf16),
        turn.astype(np.float32),
    )


def dot(a, b):
    return jnp.dot(a, b, preferred_element_type=jnp.float32)


def kernel(
    scale,
    x_ref, alive_ref, trend_ref, level_ref, table_ref, smooth_ref, turn_ref,
    out_ref,
    halo, cbuf, kbuf, rot, acc, part_out, part_in,
    halo_send, halo_recv, c_send, c_recv, k_send, k_recv, part_send, part_recv,
):
    rows = x_ref.shape[0]
    half = rows // 2
    chan = lax.axis_index("chan")
    win = lax.axis_index("win")
    x, yl, co = chan // 4, (chan // 2) % 2, chan % 2
    yh, z = win // 8, win % 8
    z2, z1, z0 = z // 4, (z // 2) % 2, z % 2

    chan_xp = ((x + 1) % 4) * 4 + yl * 2 + co
    chan_xm = ((x + 3) % 4) * 4 + yl * 2 + co
    chan_yo = x * 4 + (1 - yl) * 2 + co
    chan_co = x * 4 + yl * 2 + (1 - co)
    win_r = yh * 8 + (z + 1) % 8
    win_l = yh * 8 + (z + 7) % 8
    win_other = (1 - yh) * 8 + z
    win_next = (win + 1) % 16
    win_prev = (win + 15) % 16

    barrier = pltpu.get_barrier_semaphore()
    for device in (
        (chan, win_r), (chan, win_l), (chan, win_next), (chan, win_prev), (chan, win_other),
        (chan_xp, win), (chan_xm, win), (chan_yo, win), (chan_co, win),
    ):
        pl.semaphore_signal(barrier, inc=1, device_id=device, device_id_type=MESH)
    pl.semaphore_wait(barrier, 9)

    to_next = pltpu.make_async_remote_copy(
        src_ref=x_ref.at[:, SEG - 128 : SEG], dst_ref=halo.at[0],
        send_sem=halo_send.at[0], recv_sem=halo_recv.at[0],
        device_id=(chan, win_next), device_id_type=MESH,
    )
    to_prev = pltpu.make_async_remote_copy(
        src_ref=x_ref.at[:, 0:128], dst_ref=halo.at[1],
        send_sem=halo_send.at[1], recv_sem=halo_recv.at[1],
        device_id=(chan, win_prev), device_id_type=MESH,
    )

    @pl.when(win < 15)
    def _():
        to_next.start()

    @pl.when(win > 0)
    def _():
        to_prev.start()

    acc[...] = jnp.zeros_like(acc)

    @pl.when(win > 0)
    def _():
        to_next.wait_recv()

    @pl.when(win == 0)
    def _():
        halo[0] = jnp.zeros_like(halo[0])

    @pl.when(win < 15)
    def _():
        to_prev.wait_recv()

    @pl.when(win == 15)
    def _():
        halo[1] = jnp.zeros_like(halo[1])

    def whiten(h):
        here = pl.ds(h * half, half)
        lines = x_ref[here, :]
        pieces = [
            dot(halo[0, here, :], trend_ref[128:256, :]) + dot(lines[:, 0:256], trend_ref[256:512, :])
        ]
        for p in range(3):
            pieces.append(dot(lines[:, 256 * p : 256 * p + 512], trend_ref[...]))
        pieces.append(
            dot(lines[:, 768:1024], trend_ref[0:256, :]) + dot(halo[1, here, :], trend_ref[256:384, :])
        )
        detrended = jnp.concatenate(pieces, axis=1)
        size = jnp.abs(detrended)
        high = size.astype(jnp.bfloat16)
        low = (size - high.astype(jnp.float32)).astype(jnp.bfloat16)
        spectra = jnp.zeros((half, 2 * NF), jnp.float32)
        for q in range(4):
            window = slice(256 * q, 256 * q + 512)
            total = dot(high[:, window], level_ref[...]) + dot(low[:, window], level_ref[...])
            middle = detrended[:, 128 + 256 * q : 384 + 256 * q]
            normal = middle * float(LEVEL) / (total + float(LEVEL * TREND * 1e-05))
            spectra += dot(normal.astype(jnp.bfloat16), table_ref[256 * q : 256 * q + 256, :])
        re, im = spectra[:, :NF], spectra[:, NF:]
        size = jnp.sqrt(re * re + im * im)
        high = size.astype(jnp.bfloat16)
        low = (size - high.astype(jnp.float32)).astype(jnp.bfloat16)
        sums = dot(high, smooth_ref[...]) + dot(low, smooth_ref[...])
        level = sums[:, :NF] * (1.0 / SMOOTH) + sums[:, NF:] * (1.0 / NF) + 1e-05
        factor = alive_ref[here, :] / level
        white = jnp.concatenate([re * factor, im * factor], axis=1)
        cbuf[0, h] = white.astype(jnp.bfloat16)

    def ring(p, u, v, h=None):
        source = cbuf.at[u, p if h is None else h]
        return pltpu.make_async_remote_copy(
            src_ref=source, dst_ref=cbuf.at[v, p],
            send_sem=c_send.at[v, p], recv_sem=c_recv.at[v, p],
            device_id=(chan, (win_r, win_l)[p]), device_id_type=MESH,
        )

    targets = (chan_co, chan_xp, chan_xm, chan_yo)

    def spread(source, s, n, p, target):
        return pltpu.make_async_remote_copy(
            src_ref=source, dst_ref=kbuf.at[s, n, p],
            send_sem=k_send.at[s, n, p, target], recv_sem=k_recv.at[s, n, p],
            device_id=(targets[target], win), device_id_type=MESH,
        )

    dy, dc = (yl + z1) % 2, (co + z0) % 2
    dx = [(x - ((s + yh) % 2) * 2 - z2 + 4) % 4 for s in range(2)]
    away = [d * (4 - d) for d in dx]
    depth = [a // 3 + a // 4 + dy for a in away]
    relays = dc == 0
    is_source = [jnp.logical_and(relays, depth[s] == 0) for s in range(2)]

    def sends(s, p):
        plus = dx[s] == 0
        minus = dx[s] == 0
        if p == 0:
            plus = jnp.logical_or(plus, dx[s] == 1)
        else:
            minus = jnp.logical_or(minus, dx[s] == 3)
        up = jnp.logical_and(dx[s] == 0, dy == 0)
        return (relays, *(jnp.logical_and(relays, c) for c in (plus, minus, up)))

    def pass_on(source, s, n, p):
        for target, wanted in enumerate(sends(s, p)):
            @pl.when(wanted)
            def _():
                spread(source, s, n, p, target).start()

    def own(s, u, p):
        return pltpu.make_async_copy(cbuf.at[u, p], kbuf.at[s, u, p], k_recv.at[s, u, p])

    def arrived(s, n, p):
        pltpu.make_async_copy(kbuf.at[s, n, p], kbuf.at[s, n, p], k_recv.at[s, n, p]).wait()

    def source_step(u, p):
        for s in range(2):
            @pl.when(is_source[s])
            def _():
                pass_on(cbuf.at[u, p], s, u, p)
                own(s, u, p).start()

    def relay_step(u):
        for p in range(2):
            for s in range(2):
                n = u - depth[s]

                @pl.when((n >= 0) & (n < STEPS) & relays & (depth[s] > 0))
                def _():
                    arrived(s, n, p)
                    pass_on(kbuf.at[s, n, p], s, n, p)

    def ready(m):
        for p in range(2):
            for s in range(2):
                @pl.when(jnp.logical_or(jnp.logical_not(relays), is_source[s]))
                def _():
                    arrived(s, m, p)

    cos, sin = turn_ref[0:1, :], turn_ref[1:2, :]

    def correlate(places):
        for h, (u, p) in enumerate(places):
            block = cbuf[u, p].astype(jnp.float32)
            re, im = block[:, :NF], block[:, NF:]
            rc, rs, ic, iss = re * cos, re * sin, im * cos, im * sin
            for lag, (a, b) in enumerate(((rc + iss, ic - rs), (rc - iss, ic + rs))):
                rot[pl.ds(lag * rows + h * half, half), :NF] = a.astype(jnp.bfloat16)
                rot[pl.ds(lag * rows + h * half, half), NF:] = b.astype(jnp.bfloat16)
        for s in (1, 0):
            for h, (u, p) in enumerate(places):
                acc[s, pl.ds(h * half, half), :] += lax.dot_general(
                    kbuf[s, u, p], rot[...], (((1,), (1,)), ((), ())),
                    preferred_element_type=jnp.float32,
                )

    for u in range(STEPS + DEEPEST):
        if u == 0:
            for h in range(2):
                whiten(h)
                ring(0, 0, 1 + h, h).start()
                ring(1, 0, 1 + h, h).start()
                source_step(0, h)
        elif u < STEPS:
            for p in range(2):
                ring(p, 0, u).wait_recv()
                if u < 5:
                    ring(p, u, u + 2).start()
                elif u == 5 + p:
                    ring(p, u, 7).start()
                source_step(u, p)
        relay_step(u)
        m = u - DEEPEST
        if m >= 0:
            ready(m)
            if m in (0, 7):
                correlate([(m, 0), (m, 1)])
            elif m % 2 == 0:
                for p in range(2):
                    correlate([(m - 1, p), (m, p)])

    part_out[...] = acc[1].astype(jnp.bfloat16)
    partial = pltpu.make_async_remote_copy(
        src_ref=part_out, dst_ref=part_in, send_sem=part_send, recv_sem=part_recv,
        device_id=(chan, win_other), device_id_type=MESH,
    )
    partial.start()

    @pl.when(win < 15)
    def _():
        to_next.wait_send()

    @pl.when(win > 0)
    def _():
        to_prev.wait_send()

    for h in range(2):
        ring(0, 0, 1 + h, h).wait_send()
        ring(1, 0, 1 + h, h).wait_send()
    for p in range(2):
        for v in range(3, STEPS):
            ring(p, 0, v).wait_send()
    for s in range(2):
        for p in range(2):
            for target, wanted in enumerate(sends(s, p)):
                @pl.when(wanted)
                def _():
                    @pl.loop(0, STEPS)
                    def _(n):
                        spread(kbuf.at[s, n, p], s, n, p, target).wait_send()
    partial.wait_send()
    partial.wait_recv()
    out_ref[...] = (acc[0] + part_in[...].astype(jnp.float32)) * scale


def local(strain, alive_flags):
    rows = strain.shape[0]
    half = rows // 2
    scale = 1.0 / math.sqrt(NF * lax.axis_size("win"))
    vmem = pl.BlockSpec(memory_space=pltpu.VMEM)
    dma = pltpu.SemaphoreType.DMA
    stacked = pl.pallas_call(
        functools.partial(kernel, scale),
        out_shape=jax.ShapeDtypeStruct((rows, LAGS * rows), jnp.float32),
        in_specs=[vmem] * 7,
        out_specs=vmem,
        scratch_shapes=[
            pltpu.VMEM((2, rows, 128), jnp.bfloat16),
            pltpu.VMEM((STEPS, 2, half, 2 * NF), jnp.bfloat16),
            pltpu.VMEM((2, STEPS, 2, half, 2 * NF), jnp.bfloat16),
            pltpu.VMEM((LAGS * rows, 2 * NF), jnp.bfloat16),
            pltpu.VMEM((2, rows, LAGS * rows), jnp.float32),
            pltpu.VMEM((rows, LAGS * rows), jnp.bfloat16),
            pltpu.VMEM((rows, LAGS * rows), jnp.bfloat16),
            dma((2,)), dma((2,)),
            dma((STEPS, 2)), dma((STEPS, 2)),
            dma((2, STEPS, 2, 4)), dma((2, STEPS, 2)),
            dma, dma,
        ],
        compiler_params=pltpu.CompilerParams(
            collective_id=0, has_side_effects=True, vmem_limit_bytes=40 * 1024 * 1024
        ),
        cost_estimate=pl.CostEstimate(
            flops=3_000_000_000, bytes_accessed=4_000_000, transcendentals=0
        ),
    )(strain, alive_flags.astype(jnp.float32)[:, None], *constants())
    return stacked.reshape(rows, LAGS, rows)


def solution(mesh):
    return jax.shard_map(
        local,
        mesh=mesh,
        in_specs=(P("chan", "win"), P("chan")),
        out_specs=P("win", None, "chan"),
        check_vma=False,
    )
```

```python
import functools
import math

import jax
import jax.numpy as jnp
import ml_dtypes
import numpy as np
from jax import lax
from jax.experimental import pallas as pl
from jax.experimental.pallas import tpu as pltpu
from jax.sharding import PartitionSpec as P

NF = 256
FIRST_BIN = 64
SEG = 1024
TREND_REACH = 8
LEVEL_REACH = 32
BIN_REACH = 4
LAGS = 2
MESH = pl.DeviceIdType.MESH

TREND = 2 * TREND_REACH + 1
LEVEL = 2 * LEVEL_REACH + 1
SMOOTH = 2 * BIN_REACH + 1
STEPS = 8


def constants():
    bf16 = ml_dtypes.bfloat16
    off = np.arange(512)[:, None] - 128 - np.arange(256)[None, :]
    trend = TREND * (off == 0) - 1.0 * (np.abs(off) <= TREND_REACH)
    level = 1.0 * (np.abs(off) <= LEVEL_REACH)
    k = np.arange(SEG)[:, None]
    f = np.arange(NF)[None, :] + FIRST_BIN
    angle = 2.0 * math.pi / SEG * (k * f % SEG)
    table = np.concatenate([np.cos(angle), -np.sin(angle)], axis=1)
    bins = np.arange(NF)
    near = 1.0 * (np.abs(bins[:, None] - bins[None, :]) <= BIN_REACH)
    smooth = np.concatenate([near, np.ones((NF, NF))], axis=1)
    theta = 2.0 * math.pi / SEG * (f * 2 % SEG)
    turn = np.concatenate([np.cos(theta), np.sin(theta)], axis=0)
    turn = np.concatenate([turn, np.zeros((6, NF))], axis=0)
    return (
        trend.astype(bf16),
        level.astype(bf16),
        table.astype(bf16),
        smooth.astype(bf16),
        turn.astype(np.float32),
    )


def dot(a, b):
    return jnp.dot(a, b, preferred_element_type=jnp.float32)


def kernel(
    scale,
    x_hbm, alive_hbm, trend_hbm, level_hbm, table_hbm, smooth_hbm, turn_hbm,
    out_ref,
    x_ref, alive_ref, trend_ref, level_ref, table_ref, smooth_ref, turn_ref, load_sem,
    halo, cbuf, moved, kbuf, rot, acc, part_out, part_in,
    halo_send, halo_recv, c_send, c_recv, m_send, m_recv, s_send, s_recv, k_send, k_recv, part_send, part_recv,
):
    rows = x_ref.shape[0]
    half = rows // 2
    loads = [
        pltpu.make_async_copy(source, held, load_sem.at[i])
        for i, (source, held) in enumerate((
            (x_hbm, x_ref), (trend_hbm, trend_ref), (level_hbm, level_ref), (table_hbm, table_ref),
            (smooth_hbm, smooth_ref), (alive_hbm, alive_ref), (turn_hbm, turn_ref),
        ))
    ]
    for load in loads:
        load.start()
    chan = lax.axis_index("chan")
    win = lax.axis_index("win")
    x, yl, co = chan // 4, (chan // 2) % 2, chan % 2
    yh, z = win // 8, win % 8
    z2, z1, z0 = z // 4, (z // 2) % 2, z % 2

    chan_xp = ((x + 1) % 4) * 4 + yl * 2 + co
    chan_xm = ((x + 3) % 4) * 4 + yl * 2 + co
    chan_yo = x * 4 + (1 - yl) * 2 + co
    chan_co = x * 4 + yl * 2 + (1 - co)
    win_r = yh * 8 + (z + 1) % 8
    win_l = yh * 8 + (z + 7) % 8
    win_other = (1 - yh) * 8 + z
    win_next = (win + 1) % 16
    win_prev = (win + 15) % 16

    chan_x2 = ((x + 2) % 4) * 4 + yl * 2 + co
    column, pair = (chan // 2) % 4, z // 2
    base = (chan // 8) * 8

    def xor(a, b):
        return (a // 2 + b // 2) % 2 * 2 + (a + b) % 2

    via = [xor(xor(column, pair), 2 * h + co) for h in range(2)]
    via_chan = [base + 2 * via[h] + co for h in range(2)]
    moves = [via[h] != column for h in range(2)]
    swap_chan = base + 2 * column + z0
    swap_win = [yh * 8 + 2 * via[h] + co for h in range(2)]
    giver_chan = base + 2 * column + z0
    giver_win = [yh * 8 + 2 * xor(xor(column, pair), 2 * h + z0) + co for h in range(2)]
    swaps = [2 * via[h] + co != z for h in range(2)]

    barrier = pltpu.get_barrier_semaphore()
    for device in (
        (chan, win_r), (chan, win_l), (chan, win_next), (chan, win_prev), (chan, win_other),
        (chan_xp, win), (chan_xm, win), (chan_x2, win), (chan_yo, win), (chan_co, win),
    ):
        pl.semaphore_signal(barrier, inc=1, device_id=device, device_id_type=MESH)

    for h in range(2):
        @pl.when(2 * xor(xor(column, pair), 2 * h + z0) + co != z)
        def _():
            pl.semaphore_signal(barrier, inc=1, device_id=(giver_chan, giver_win[h]), device_id_type=MESH)

        @pl.when(moves[h])
        def _():
            pl.semaphore_signal(barrier, inc=1, device_id=(via_chan[h], win), device_id_type=MESH)

    pl.semaphore_wait(barrier, 10 + sum(w.astype(jnp.int32) for w in (*swaps, *moves)))

    to_next = pltpu.make_async_remote_copy(
        src_ref=x_hbm.at[:, SEG - 128 : SEG], dst_ref=halo.at[0],
        send_sem=halo_send.at[0], recv_sem=halo_recv.at[0],
        device_id=(chan, win_next), device_id_type=MESH,
    )
    to_prev = pltpu.make_async_remote_copy(
        src_ref=x_hbm.at[:, 0:128], dst_ref=halo.at[1],
        send_sem=halo_send.at[1], recv_sem=halo_recv.at[1],
        device_id=(chan, win_prev), device_id_type=MESH,
    )

    @pl.when(win < 15)
    def _():
        to_next.start()

    @pl.when(win > 0)
    def _():
        to_prev.start()

    for load in loads:
        load.wait()

    @pl.when(win > 0)
    def _():
        to_next.wait_recv()

    @pl.when(win == 0)
    def _():
        halo[0] = jnp.zeros_like(halo[0])

    @pl.when(win < 15)
    def _():
        to_prev.wait_recv()

    @pl.when(win == 15)
    def _():
        halo[1] = jnp.zeros_like(halo[1])

    def whiten(h):
        here = pl.ds(h * half, half)
        lines = x_ref[here, :]
        pieces = [
            dot(halo[0, here, :], trend_ref[128:256, :]) + dot(lines[:, 0:256], trend_ref[256:512, :])
        ]
        for p in range(3):
            pieces.append(dot(lines[:, 256 * p : 256 * p + 512], trend_ref[...]))
        pieces.append(
            dot(lines[:, 768:1024], trend_ref[0:256, :]) + dot(halo[1, here, :], trend_ref[256:384, :])
        )
        detrended = jnp.concatenate(pieces, axis=1)
        size = jnp.abs(detrended)
        high = size.astype(jnp.bfloat16)
        low = (size - high.astype(jnp.float32)).astype(jnp.bfloat16)
        spectra = jnp.zeros((half, 2 * NF), jnp.float32)
        for q in range(4):
            window = slice(256 * q, 256 * q + 512)
            total = dot(high[:, window], level_ref[...]) + dot(low[:, window], level_ref[...])
            middle = detrended[:, 128 + 256 * q : 384 + 256 * q]
            normal = middle * float(LEVEL) / (total + float(LEVEL * TREND * 1e-05))
            spectra += dot(normal.astype(jnp.bfloat16), table_ref[256 * q : 256 * q + 256, :])
        re, im = spectra[:, :NF], spectra[:, NF:]
        size = jnp.sqrt(re * re + im * im)
        high = size.astype(jnp.bfloat16)
        low = (size - high.astype(jnp.float32)).astype(jnp.bfloat16)
        sums = dot(high, smooth_ref[...]) + dot(low, smooth_ref[...])
        level = sums[:, :NF] * (1.0 / SMOOTH) + sums[:, NF:] * (1.0 / NF) + 1e-05
        flags = jnp.broadcast_to(alive_ref[h : h + 1, :], (half, half))
        place = [lax.broadcasted_iota(jnp.int32, (half, half), d) for d in range(2)]
        flags = jnp.where(place[0] == place[1], flags, 0).astype(jnp.float32)
        factor = jnp.sum(flags, axis=1, keepdims=True) / level
        white = jnp.concatenate([re * factor, im * factor], axis=1)
        cbuf[z, h] = white.astype(jnp.bfloat16)

    def ring(p, t, h):
        source = (z + (8 - t, t)[p]) % 8
        return pltpu.make_async_remote_copy(
            src_ref=cbuf.at[source, h], dst_ref=cbuf.at[source, h],
            send_sem=c_send.at[p, t, h], recv_sem=c_recv.at[source, h],
            device_id=(chan, (win_r, win_l)[p]), device_id_type=MESH,
        )

    def ring_arrived(p, t, h):
        source = (z + (8 - t, t)[p]) % 8
        here = cbuf.at[source, h]
        pltpu.make_async_copy(here, here, c_recv.at[source, h]).wait()

    def ring_step(u):
        t = (u + 1) // 2
        for p in range(2):
            h = p if t == 4 else (u + 1) % 2
            ring_arrived(p, t, h)
            if t < 3 or (t == 3 and h == p):
                ring(p, t, h).start()

    def aside(h):
        return pltpu.make_async_remote_copy(
            src_ref=cbuf.at[z, h], dst_ref=moved.at[h],
            send_sem=m_send.at[h], recv_sem=m_recv.at[h],
            device_id=(via_chan[h], win), device_id_type=MESH,
        )

    def swap(source, h):
        return pltpu.make_async_remote_copy(
            src_ref=source, dst_ref=kbuf.at[base + z, h],
            send_sem=s_send.at[h], recv_sem=s_recv.at[h],
            device_id=(swap_chan, swap_win[h]), device_id_type=MESH,
        )

    def held_by(c, h):
        return (c // 8) * 8 + 2 * xor(xor((c // 2) % 4, pair), 2 * h + z0) + c % 2

    def keep(source, h):
        return pltpu.make_async_copy(source, kbuf.at[base + z, h], s_recv.at[h])

    def onward(source, h):
        @pl.when(swaps[h])
        def _():
            swap(source, h).start()

        @pl.when(jnp.logical_not(swaps[h]))
        def _():
            keep(source, h).start()

    def row_other(c):
        return c + 2 - 4 * ((c // 2) % 2)

    def core_other(c):
        return c + 1 - 2 * (c % 2)

    blocks = (
        chan, chan_yo, chan_xp, chan_xm, chan_x2,
        row_other(chan_xp), row_other(chan_xm), row_other(chan_x2),
    )
    targets = (chan_co, chan_xp, chan_xm, chan_x2, chan_yo)

    def spread(b, h, target):
        held = kbuf.at[held_by(blocks[b], h), h]
        return pltpu.make_async_remote_copy(
            src_ref=held, dst_ref=held,
            send_sem=k_send.at[b, h, target], recv_sem=k_recv.at[blocks[b], h],
            device_id=(targets[target], win), device_id_type=MESH,
        )

    def goes_to(b, h):
        if b == 0:
            return (1, 2, 3, 4, 0)
        if b == 1:
            return (1, 2, 3, 0) if h == 0 else (0,)
        if b < 5:
            return (4, 0) if h == 1 else (0,)
        return (0,)

    def arrived(c, h):
        held = kbuf.at[held_by(c, h), h]
        pltpu.make_async_copy(held, held, k_recv.at[c, h]).wait()

    def pass_on(b, h):
        if b == 0:
            held = kbuf.at[held_by(chan, h), h]
            pltpu.make_async_copy(held, held, s_recv.at[h]).wait()
        else:
            arrived(blocks[b], h)
        for target in goes_to(b, h):
            spread(b, h, target).start()

    cos, sin = turn_ref[0:1, :], turn_ref[1:2, :]

    def turn(source):
        for h in range(2):
            block = cbuf[source, h].astype(jnp.float32)
            re, im = block[:, :NF], block[:, NF:]
            rc, rs, ic, iss = re * cos, re * sin, im * cos, im * sin
            for lag, (a, b) in enumerate(((rc + iss, ic - rs), (rc - iss, ic + rs))):
                here = pl.ds(lag * rows + h * half, half)
                rot[source, here, :NF] = a.astype(jnp.bfloat16)
                rot[source, here, NF:] = b.astype(jnp.bfloat16)

    def product(which, lag):
        total = jnp.zeros((rows, rows), jnp.float32)
        for seg in range(STEPS):
            total += lax.dot_general(
                kbuf[which * 8 + seg].reshape(rows, 2 * NF), rot[seg, pl.ds(lag * rows, rows), :],
                (((1,), (1,)), ((), ())), preferred_element_type=jnp.float32,
            )
        return total

    def partial(h):
        return pltpu.make_async_remote_copy(
            src_ref=part_out.at[h], dst_ref=part_in.at[h],
            send_sem=part_send.at[h], recv_sem=part_recv.at[h],
            device_id=(chan, win_other), device_id_type=MESH,
        )

    for h in range(2):
        whiten(h)

        @pl.when(moves[h])
        def _():
            aside(h).start()

        @pl.when(jnp.logical_not(moves[h]))
        def _():
            onward(cbuf.at[z, h], h)

        ring(0, 0, h).start()
        ring(1, 0, h).start()

    for h in range(2):
        @pl.when(moves[h])
        def _():
            aside(h).wait_recv()
            onward(moved.at[h], h)

    turn(z)
    ring_step(1)
    ring_step(2)
    turn((z + 7) % 8)
    turn((z + 1) % 8)
    pass_on(0, 0)
    pass_on(0, 1)
    ring_step(3)
    pass_on(1, 0)
    pass_on(1, 1)
    ring_step(4)
    turn((z + 6) % 8)
    turn((z + 2) % 8)
    pass_on(2, 1)
    pass_on(3, 1)
    pass_on(4, 1)
    ring_step(5)
    pass_on(2, 0)
    pass_on(3, 0)
    pass_on(4, 0)
    ring_step(6)
    turn((z + 5) % 8)
    turn((z + 3) % 8)
    pass_on(5, 0)
    pass_on(6, 0)
    pass_on(7, 0)
    ring_step(7)
    turn((z + 4) % 8)
    pass_on(5, 1)
    pass_on(6, 1)
    pass_on(7, 1)
    for h in range(2):
        for b in range(8):
            arrived(core_other(blocks[b]), h)

    for h in range(2):
        part_out[h] = product(1 - yh, h).astype(jnp.bfloat16)
        partial(h).start()
    for h in range(2):
        acc[h] = product(yh, h)

    @pl.when(win < 15)
    def _():
        to_next.wait_send()

    @pl.when(win > 0)
    def _():
        to_prev.wait_send()

    for h in range(2):
        @pl.when(swaps[h])
        def _():
            swap(moved.at[h], h).wait_send()

        @pl.when(moves[h])
        def _():
            aside(h).wait_send()

        for p in range(2):
            for t in range(4 if h == p else 3):
                ring(p, t, h).wait_send()
        for b in range(8):
            for target in goes_to(b, h):
                spread(b, h, target).wait_send()
    for h in range(2):
        partial(h).wait_send()
        partial(h).wait_recv()
        out_ref[:, pl.ds(h * rows, rows)] = (acc[h] + part_in[h].astype(jnp.float32)) * scale


def local(strain, alive_flags):
    rows = strain.shape[0]
    half = rows // 2
    scale = 1.0 / math.sqrt(NF * lax.axis_size("win"))
    vmem = pl.BlockSpec(memory_space=pltpu.VMEM)
    tables = constants()
    dma = pltpu.SemaphoreType.DMA
    stacked = pl.pallas_call(
        functools.partial(kernel, scale),
        out_shape=jax.ShapeDtypeStruct((rows, LAGS * rows), jnp.float32),
        in_specs=[pl.BlockSpec(memory_space=pltpu.HBM)] * 7,
        out_specs=vmem,
        scratch_shapes=[
            pltpu.VMEM(strain.shape, jnp.bfloat16),
            pltpu.VMEM((2, half), jnp.int32),
            *(pltpu.VMEM(t.shape, t.dtype) for t in tables),
            dma((7,)),
            pltpu.VMEM((2, rows, 128), jnp.bfloat16),
            pltpu.VMEM((STEPS, 2, half, 2 * NF), jnp.bfloat16),
            pltpu.VMEM((2, half, 2 * NF), jnp.bfloat16),
            pltpu.VMEM((2 * STEPS, 2, half, 2 * NF), jnp.bfloat16),
            pltpu.VMEM((STEPS, LAGS * rows, 2 * NF), jnp.bfloat16),
            pltpu.VMEM((LAGS, rows, rows), jnp.float32),
            pltpu.VMEM((LAGS, rows, rows), jnp.bfloat16),
            pltpu.VMEM((LAGS, rows, rows), jnp.bfloat16),
            dma((2,)), dma((2,)),
            dma((2, 4, 2)), dma((STEPS, 2)),
            dma((2,)), dma((2,)),
            dma((2,)), dma((2,)),
            dma((8, 2, 5)), dma((2 * STEPS, 2)),
            dma((2,)), dma((2,)),
        ],
        compiler_params=pltpu.CompilerParams(
            collective_id=0, has_side_effects=True, vmem_limit_bytes=63 * 1024 * 1024
        ),
        cost_estimate=pl.CostEstimate(
            flops=3_000_000_000, bytes_accessed=4_000_000, transcendentals=0
        ),
    )(strain, alive_flags.reshape(2, half), *tables)
    return stacked.reshape(rows, LAGS, rows)


def solution(mesh):
    return jax.shard_map(
        local,
        mesh=mesh,
        in_specs=(P("chan", "win"), P("chan")),
        out_specs=P("win", None, "chan"),
        check_vma=False,
    )
```

```python
import functools
import math

import jax
import jax.numpy as jnp
import ml_dtypes
import numpy as np
from jax import lax
from jax.experimental import pallas as pl
from jax.experimental.pallas import tpu as pltpu
from jax.sharding import PartitionSpec as P

NF = 256
FIRST_BIN = 64
SEG = 1024
TREND_REACH = 8
LEVEL_REACH = 32
BIN_REACH = 4
LAGS = 2
MESH = pl.DeviceIdType.MESH

TREND = 2 * TREND_REACH + 1
LEVEL = 2 * LEVEL_REACH + 1
SMOOTH = 2 * BIN_REACH + 1
STEPS = 8


def constants():
    bf16 = ml_dtypes.bfloat16
    off = np.arange(512)[:, None] - 128 - np.arange(256)[None, :]
    trend = TREND * (off == 0) - 1.0 * (np.abs(off) <= TREND_REACH)
    level = 1.0 * (np.abs(off) <= LEVEL_REACH)
    k = np.arange(SEG)[:, None]
    f = np.arange(NF)[None, :] + FIRST_BIN
    angle = 2.0 * math.pi / SEG * (k * f % SEG)
    table = np.concatenate([np.cos(angle), -np.sin(angle)], axis=1)
    bins = np.arange(NF)
    near = 1.0 * (np.abs(bins[:, None] - bins[None, :]) <= BIN_REACH)
    smooth = np.concatenate([near, np.ones((NF, NF))], axis=1)
    theta = 2.0 * math.pi / SEG * (f * 2 % SEG)
    turn = np.concatenate([np.cos(theta), np.sin(theta)], axis=0)
    turn = np.concatenate([turn, np.zeros((6, NF))], axis=0)
    return (
        trend.astype(bf16),
        level.astype(bf16),
        table.astype(bf16),
        smooth.astype(bf16),
        turn.astype(np.float32),
    )


def dot(a, b):
    return jnp.dot(a, b, preferred_element_type=jnp.float32)


def kernel(
    scale,
    x_hbm, alive_hbm, trend_hbm, level_hbm, table_hbm, smooth_hbm, turn_hbm,
    out_ref,
    x_ref, alive_ref, trend_ref, level_ref, table_ref, smooth_ref, turn_ref, load_sem,
    halo, cbuf, moved, kbuf, rot, acc, part_out, part_in,
    halo_send, halo_recv, c_send, c_recv, m_send, m_recv, s_send, s_recv, k_send, k_recv, part_send, part_recv,
):
    rows = x_ref.shape[0]
    half = rows // 2
    loads = [
        pltpu.make_async_copy(source, held, load_sem.at[i])
        for i, (source, held) in enumerate((
            (x_hbm, x_ref), (trend_hbm, trend_ref), (level_hbm, level_ref), (table_hbm, table_ref),
            (smooth_hbm, smooth_ref), (alive_hbm, alive_ref), (turn_hbm, turn_ref),
        ))
    ]
    for load in loads:
        load.start()
    chan = lax.axis_index("chan")
    win = lax.axis_index("win")
    x, yl, co = chan // 4, (chan // 2) % 2, chan % 2
    yh, z = win // 8, win % 8
    z2, z1, z0 = z // 4, (z // 2) % 2, z % 2

    chan_xp = ((x + 1) % 4) * 4 + yl * 2 + co
    chan_xm = ((x + 3) % 4) * 4 + yl * 2 + co
    chan_yo = x * 4 + (1 - yl) * 2 + co
    chan_co = x * 4 + yl * 2 + (1 - co)
    win_r = yh * 8 + (z + 1) % 8
    win_l = yh * 8 + (z + 7) % 8
    win_other = (1 - yh) * 8 + z
    win_next = (win + 1) % 16
    win_prev = (win + 15) % 16

    chan_x2 = ((x + 2) % 4) * 4 + yl * 2 + co
    column, pair = (chan // 2) % 4, z // 2
    base = (chan // 8) * 8

    def xor(a, b):
        return (a // 2 + b // 2) % 2 * 2 + (a + b) % 2

    via = [xor(xor(column, pair), 2 * h + co) for h in range(2)]
    via_chan = [base + 2 * via[h] + co for h in range(2)]
    moves = [via[h] != column for h in range(2)]
    swap_chan = base + 2 * column + z0
    swap_win = [yh * 8 + 2 * via[h] + co for h in range(2)]
    giver_chan = base + 2 * column + z0
    giver_win = [yh * 8 + 2 * xor(xor(column, pair), 2 * h + z0) + co for h in range(2)]
    swaps = [2 * via[h] + co != z for h in range(2)]

    barrier = pltpu.get_barrier_semaphore()
    for device in (
        (chan, win_r), (chan, win_l), (chan, win_next), (chan, win_prev), (chan, win_other),
        (chan_xp, win), (chan_xm, win), (chan_x2, win), (chan_yo, win), (chan_co, win),
    ):
        pl.semaphore_signal(barrier, inc=1, device_id=device, device_id_type=MESH)

    for h in range(2):
        @pl.when(2 * xor(xor(column, pair), 2 * h + z0) + co != z)
        def _():
            pl.semaphore_signal(barrier, inc=1, device_id=(giver_chan, giver_win[h]), device_id_type=MESH)

        @pl.when(moves[h])
        def _():
            pl.semaphore_signal(barrier, inc=1, device_id=(via_chan[h], win), device_id_type=MESH)

    pl.semaphore_wait(barrier, 10 + sum(w.astype(jnp.int32) for w in (*swaps, *moves)))

    to_next = pltpu.make_async_remote_copy(
        src_ref=x_hbm.at[:, SEG - 128 : SEG], dst_ref=halo.at[0],
        send_sem=halo_send.at[0], recv_sem=halo_recv.at[0],
        device_id=(chan, win_next), device_id_type=MESH,
    )
    to_prev = pltpu.make_async_remote_copy(
        src_ref=x_hbm.at[:, 0:128], dst_ref=halo.at[1],
        send_sem=halo_send.at[1], recv_sem=halo_recv.at[1],
        device_id=(chan, win_prev), device_id_type=MESH,
    )

    @pl.when(win < 15)
    def _():
        to_next.start()

    @pl.when(win > 0)
    def _():
        to_prev.start()

    for load in loads:
        load.wait()

    def split(value):
        high = value.astype(jnp.bfloat16)
        return high, (value - high.astype(jnp.float32)).astype(jnp.bfloat16)

    def spectra_of(pieces, q):
        middle = jnp.concatenate(pieces, axis=1)
        high, low = split(jnp.abs(middle))
        total = dot(high, level_ref[...]) + dot(low, level_ref[...])
        normal = middle[:, 128:384] * float(LEVEL) / (total + float(LEVEL * TREND * 1e-05))
        return dot(normal.astype(jnp.bfloat16), table_ref[256 * q : 256 * q + 256, :])

    def inside(h):
        lines = x_ref[pl.ds(h * half, half), :]
        pieces = []
        for p in range(3):
            both = dot(lines[:, 256 * p : 256 * p + 512], trend_ref[...])
            pieces += [both[:, :128], both[:, 128:]]
        return pieces, spectra_of(pieces[0:4], 1) + spectra_of(pieces[2:6], 2)

    def whiten(h, pieces, spectra):
        here = pl.ds(h * half, half)
        first = dot(halo[0, here, :], trend_ref[128:256, :]) + dot(x_ref[here, 0:256], trend_ref[256:512, :])
        last = dot(x_ref[here, 768:1024], trend_ref[0:256, :]) + dot(halo[1, here, :], trend_ref[256:384, :])
        spectra += spectra_of([first] + pieces[0:2], 0) + spectra_of(pieces[4:6] + [last], 3)
        re, im = spectra[:, :NF], spectra[:, NF:]
        size = jnp.sqrt(re * re + im * im)
        high, low = split(size)
        sums = dot(high, smooth_ref[...]) + dot(low, smooth_ref[...])
        level = sums[:, :NF] * (1.0 / SMOOTH) + sums[:, NF:] * (1.0 / NF) + 1e-05
        flags = jnp.broadcast_to(alive_ref[h : h + 1, :], (half, half))
        place = [lax.broadcasted_iota(jnp.int32, (half, half), d) for d in range(2)]
        flags = jnp.where(place[0] == place[1], flags, 0).astype(jnp.float32)
        factor = jnp.sum(flags, axis=1, keepdims=True) / level
        white = jnp.concatenate([re * factor, im * factor], axis=1)
        cbuf[z, h] = white.astype(jnp.bfloat16)

    def ring(p, t, h):
        source = (z + (8 - t, t)[p]) % 8
        return pltpu.make_async_remote_copy(
            src_ref=cbuf.at[source, h], dst_ref=cbuf.at[source, h],
            send_sem=c_send.at[p, t, h], recv_sem=c_recv.at[source, h],
            device_id=(chan, (win_r, win_l)[p]), device_id_type=MESH,
        )

    def ring_arrived(p, t, h):
        source = (z + (8 - t, t)[p]) % 8
        here = cbuf.at[source, h]
        pltpu.make_async_copy(here, here, c_recv.at[source, h]).wait()

    def ring_step(u):
        t = (u + 1) // 2
        for p in range(2):
            h = p if t == 4 else (u + 1) % 2
            ring_arrived(p, t, h)
            if t < 3 or (t == 3 and h == p):
                ring(p, t, h).start()

    def aside(h):
        return pltpu.make_async_remote_copy(
            src_ref=cbuf.at[z, h], dst_ref=moved.at[h],
            send_sem=m_send.at[h], recv_sem=m_recv.at[h],
            device_id=(via_chan[h], win), device_id_type=MESH,
        )

    def swap(source, h):
        return pltpu.make_async_remote_copy(
            src_ref=source, dst_ref=kbuf.at[base + z, h],
            send_sem=s_send.at[h], recv_sem=s_recv.at[h],
            device_id=(swap_chan, swap_win[h]), device_id_type=MESH,
        )

    def held_by(c, h):
        return (c // 8) * 8 + 2 * xor(xor((c // 2) % 4, pair), 2 * h + z0) + c % 2

    def keep(source, h):
        return pltpu.make_async_copy(source, kbuf.at[base + z, h], s_recv.at[h])

    def onward(source, h):
        @pl.when(swaps[h])
        def _():
            swap(source, h).start()

        @pl.when(jnp.logical_not(swaps[h]))
        def _():
            keep(source, h).start()

    def row_other(c):
        return c + 2 - 4 * ((c // 2) % 2)

    def core_other(c):
        return c + 1 - 2 * (c % 2)

    blocks = (
        chan, chan_yo, chan_xp, chan_xm, chan_x2,
        row_other(chan_xp), row_other(chan_xm), row_other(chan_x2),
    )
    targets = (chan_co, chan_xp, chan_xm, chan_x2, chan_yo)

    def spread(b, h, target):
        held = kbuf.at[held_by(blocks[b], h), h]
        return pltpu.make_async_remote_copy(
            src_ref=held, dst_ref=held,
            send_sem=k_send.at[b, h, target], recv_sem=k_recv.at[blocks[b], h],
            device_id=(targets[target], win), device_id_type=MESH,
        )

    def goes_to(b, h):
        if b == 0:
            return (1, 2, 4, 0)
        if b == 1:
            return (1, 2, 3, 0) if h == 0 else (0,)
        if b == 2:
            return (2, 4, 0) if h == 1 else (0,)
        if b == 3:
            return (4, 0) if h == 1 else (1, 0)
        if b == 4:
            return (4, 0) if h == 1 else (0,)
        return (0,)

    def arrived(c, h):
        held = kbuf.at[held_by(c, h), h]
        pltpu.make_async_copy(held, held, k_recv.at[c, h]).wait()

    def pass_on(b, h):
        if b == 0:
            held = kbuf.at[held_by(chan, h), h]
            pltpu.make_async_copy(held, held, s_recv.at[h]).wait()
        else:
            arrived(blocks[b], h)
        for target in goes_to(b, h):
            spread(b, h, target).start()

    cos, sin = turn_ref[0:1, :], turn_ref[1:2, :]

    def turn(source):
        for h in range(2):
            block = cbuf[source, h].astype(jnp.float32)
            re, im = block[:, :NF], block[:, NF:]
            rc, rs, ic, iss = re * cos, re * sin, im * cos, im * sin
            for lag, (a, b) in enumerate(((rc + iss, ic - rs), (rc - iss, ic + rs))):
                here = pl.ds(lag * rows + h * half, half)
                rot[source, here, :NF] = a.astype(jnp.bfloat16)
                rot[source, here, NF:] = b.astype(jnp.bfloat16)

    def product(which, h):
        total = jnp.zeros((half, LAGS * rows), jnp.float32)
        for seg in range(STEPS):
            total += lax.dot_general(
                kbuf[which * 8 + seg, h], rot[seg], (((1,), (1,)), ((), ())),
                preferred_element_type=jnp.float32,
            )
        return total

    def partial(h):
        return pltpu.make_async_remote_copy(
            src_ref=part_out.at[h], dst_ref=part_in.at[h],
            send_sem=part_send.at[h], recv_sem=part_recv.at[h],
            device_id=(chan, win_other), device_id_type=MESH,
        )

    begun = [inside(h) for h in range(2)]

    @pl.when(win > 0)
    def _():
        to_next.wait_recv()

    @pl.when(win == 0)
    def _():
        halo[0] = jnp.zeros_like(halo[0])

    @pl.when(win < 15)
    def _():
        to_prev.wait_recv()

    @pl.when(win == 15)
    def _():
        halo[1] = jnp.zeros_like(halo[1])

    for h in range(2):
        whiten(h, *begun[h])

        @pl.when(moves[h])
        def _():
            aside(h).start()

        @pl.when(jnp.logical_not(moves[h]))
        def _():
            onward(cbuf.at[z, h], h)

        ring(0, 0, h).start()
        ring(1, 0, h).start()

    for h in range(2):
        @pl.when(moves[h])
        def _():
            aside(h).wait_recv()
            onward(moved.at[h], h)

    turn(z)
    ring_step(1)
    pass_on(0, 0)
    pass_on(0, 1)
    ring_step(2)
    turn((z + 7) % 8)
    turn((z + 1) % 8)
    ring_step(3)
    pass_on(3, 0)
    pass_on(2, 1)
    pass_on(1, 0)
    ring_step(4)
    turn((z + 6) % 8)
    turn((z + 2) % 8)
    pass_on(3, 1)
    pass_on(2, 0)
    pass_on(1, 1)
    ring_step(5)
    ring_step(6)
    turn((z + 5) % 8)
    turn((z + 3) % 8)
    pass_on(4, 0)
    pass_on(4, 1)
    pass_on(5, 0)
    pass_on(6, 0)
    pass_on(7, 0)
    pass_on(5, 1)
    pass_on(6, 1)
    ring_step(7)
    turn((z + 4) % 8)
    pass_on(7, 1)
    def finish(h):
        for b in range(8):
            arrived(core_other(blocks[b]), h)
        part_out[h] = product(1 - yh, h).astype(jnp.bfloat16)
        partial(h).start()

    finish(0)
    finish(1)
    for h in range(2):
        acc[h] = product(yh, h)

    @pl.when(win < 15)
    def _():
        to_next.wait_send()

    @pl.when(win > 0)
    def _():
        to_prev.wait_send()

    for h in range(2):
        @pl.when(swaps[h])
        def _():
            swap(moved.at[h], h).wait_send()

        @pl.when(moves[h])
        def _():
            aside(h).wait_send()

        for p in range(2):
            for t in range(4 if h == p else 3):
                ring(p, t, h).wait_send()
        for b in range(8):
            for target in goes_to(b, h):
                spread(b, h, target).wait_send()
    for h in range(2):
        partial(h).wait_send()
        partial(h).wait_recv()
        out_ref[pl.ds(h * half, half), :] = (acc[h] + part_in[h].astype(jnp.float32)) * scale


def local(strain, alive_flags):
    rows = strain.shape[0]
    half = rows // 2
    scale = 1.0 / math.sqrt(NF * lax.axis_size("win"))
    vmem = pl.BlockSpec(memory_space=pltpu.VMEM)
    tables = constants()
    dma = pltpu.SemaphoreType.DMA
    stacked = pl.pallas_call(
        functools.partial(kernel, scale),
        out_shape=jax.ShapeDtypeStruct((rows, LAGS * rows), jnp.float32),
        in_specs=[pl.BlockSpec(memory_space=pltpu.HBM)] * 7,
        out_specs=vmem,
        scratch_shapes=[
            pltpu.VMEM(strain.shape, jnp.bfloat16),
            pltpu.VMEM((2, half), jnp.int32),
            *(pltpu.VMEM(t.shape, t.dtype) for t in tables),
            dma((7,)),
            pltpu.VMEM((2, rows, 128), jnp.bfloat16),
            pltpu.VMEM((STEPS, 2, half, 2 * NF), jnp.bfloat16),
            pltpu.VMEM((2, half, 2 * NF), jnp.bfloat16),
            pltpu.VMEM((2 * STEPS, 2, half, 2 * NF), jnp.bfloat16),
            pltpu.VMEM((STEPS, LAGS * rows, 2 * NF), jnp.bfloat16),
            pltpu.VMEM((2, half, LAGS * rows), jnp.float32),
            pltpu.VMEM((2, half, LAGS * rows), jnp.bfloat16),
            pltpu.VMEM((2, half, LAGS * rows), jnp.bfloat16),
            dma((2,)), dma((2,)),
            dma((2, 4, 2)), dma((STEPS, 2)),
            dma((2,)), dma((2,)),
            dma((2,)), dma((2,)),
            dma((8, 2, 5)), dma((2 * STEPS, 2)),
            dma((2,)), dma((2,)),
        ],
        compiler_params=pltpu.CompilerParams(
            collective_id=0, has_side_effects=True, vmem_limit_bytes=63 * 1024 * 1024
        ),
        cost_estimate=pl.CostEstimate(
            flops=3_000_000_000, bytes_accessed=4_000_000, transcendentals=0
        ),
    )(strain, alive_flags.reshape(2, half), *tables)
    return stacked.reshape(rows, LAGS, rows)


def solution(mesh):
    return jax.shard_map(
        local,
        mesh=mesh,
        in_specs=(P("chan", "win"), P("chan")),
        out_specs=P("win", None, "chan"),
        check_vma=False,
    )
```

```python
import functools
import math

import jax
import jax.numpy as jnp
import ml_dtypes
import numpy as np
from jax import lax
from jax.experimental import pallas as pl
from jax.experimental.pallas import tpu as pltpu
from jax.sharding import PartitionSpec as P

NF = 256
FIRST_BIN = 64
SEG = 1024
TREND_REACH = 8
LEVEL_REACH = 32
BIN_REACH = 4
LAGS = 2
MESH = pl.DeviceIdType.MESH

TREND = 2 * TREND_REACH + 1
LEVEL = 2 * LEVEL_REACH + 1
SMOOTH = 2 * BIN_REACH + 1
STEPS = 8


def constants():
    bf16 = ml_dtypes.bfloat16
    off = np.arange(512)[:, None] - 128 - np.arange(256)[None, :]
    trend = TREND * (off == 0) - 1.0 * (np.abs(off) <= TREND_REACH)
    level = 1.0 * (np.abs(off) <= LEVEL_REACH)
    k = np.arange(SEG)[:, None]
    f = np.arange(NF)[None, :] + FIRST_BIN
    angle = 2.0 * math.pi / SEG * (k * f % SEG)
    table = np.concatenate([np.cos(angle), -np.sin(angle)], axis=1)
    bins = np.arange(NF)
    near = 1.0 * (np.abs(bins[:, None] - bins[None, :]) <= BIN_REACH)
    smooth = np.concatenate([near, np.ones((NF, NF))], axis=1)
    theta = 2.0 * math.pi / SEG * (f * 2 % SEG)
    turn = np.concatenate([np.cos(theta), np.sin(theta)], axis=0)
    turn = np.concatenate([turn, np.zeros((6, NF))], axis=0)
    return (
        trend.astype(bf16),
        level.astype(bf16),
        table.astype(bf16),
        smooth.astype(bf16),
        turn.astype(np.float32),
    )


def dot(a, b):
    return jnp.dot(a, b, preferred_element_type=jnp.float32)


def kernel(
    scale,
    x_hbm, alive_hbm, trend_hbm, level_hbm, table_hbm, smooth_hbm, turn_hbm,
    out_ref,
    x_ref, alive_ref, trend_ref, level_ref, table_ref, smooth_ref, turn_ref, load_sem,
    halo, cbuf, moved, kbuf, rot, acc, part_out, part_in,
    halo_send, halo_recv, c_send, c_recv, m_send, m_recv, s_send, s_recv, k_send, k_recv, part_send, part_recv,
):
    rows = x_ref.shape[0]
    half = rows // 2
    loads = [
        pltpu.make_async_copy(source, held, load_sem.at[i])
        for i, (source, held) in enumerate((
            (x_hbm, x_ref), (trend_hbm, trend_ref), (level_hbm, level_ref), (table_hbm, table_ref),
            (smooth_hbm, smooth_ref), (alive_hbm, alive_ref), (turn_hbm, turn_ref),
        ))
    ]
    for load in loads:
        load.start()
    chan = lax.axis_index("chan")
    win = lax.axis_index("win")
    x, yl, co = chan // 4, (chan // 2) % 2, chan % 2
    yh, z = win // 8, win % 8
    z2, z1, z0 = z // 4, (z // 2) % 2, z % 2

    chan_xp = ((x + 1) % 4) * 4 + yl * 2 + co
    chan_xm = ((x + 3) % 4) * 4 + yl * 2 + co
    chan_yo = x * 4 + (1 - yl) * 2 + co
    chan_co = x * 4 + yl * 2 + (1 - co)
    win_r = yh * 8 + (z + 1) % 8
    win_l = yh * 8 + (z + 7) % 8
    win_other = (1 - yh) * 8 + z
    win_next = (win + 1) % 16
    win_prev = (win + 15) % 16

    chan_x2 = ((x + 2) % 4) * 4 + yl * 2 + co
    column, pair = (chan // 2) % 4, z // 2
    base = (chan // 8) * 8

    def xor(a, b):
        return (a // 2 + b // 2) % 2 * 2 + (a + b) % 2

    via = [xor(xor(column, pair), 2 * h + co) for h in range(2)]
    via_chan = [base + 2 * via[h] + co for h in range(2)]
    moves = [via[h] != column for h in range(2)]
    swap_chan = base + 2 * column + z0
    swap_win = [yh * 8 + 2 * via[h] + co for h in range(2)]
    giver_chan = base + 2 * column + z0
    giver_win = [yh * 8 + 2 * xor(xor(column, pair), 2 * h + z0) + co for h in range(2)]
    swaps = [2 * via[h] + co != z for h in range(2)]

    barrier = pltpu.get_barrier_semaphore()
    for device in (
        (chan, win_r), (chan, win_l), (chan, win_next), (chan, win_prev), (chan, win_other),
        (chan_xp, win), (chan_xm, win), (chan_x2, win), (chan_yo, win), (chan_co, win),
    ):
        pl.semaphore_signal(barrier, inc=1, device_id=device, device_id_type=MESH)

    for h in range(2):
        @pl.when(2 * xor(xor(column, pair), 2 * h + z0) + co != z)
        def _():
            pl.semaphore_signal(barrier, inc=1, device_id=(giver_chan, giver_win[h]), device_id_type=MESH)

        @pl.when(moves[h])
        def _():
            pl.semaphore_signal(barrier, inc=1, device_id=(via_chan[h], win), device_id_type=MESH)

    pl.semaphore_wait(barrier, 10 + sum(w.astype(jnp.int32) for w in (*swaps, *moves)))

    to_next = pltpu.make_async_remote_copy(
        src_ref=x_hbm.at[:, SEG - 128 : SEG], dst_ref=halo.at[0],
        send_sem=halo_send.at[0], recv_sem=halo_recv.at[0],
        device_id=(chan, win_next), device_id_type=MESH,
    )
    to_prev = pltpu.make_async_remote_copy(
        src_ref=x_hbm.at[:, 0:128], dst_ref=halo.at[1],
        send_sem=halo_send.at[1], recv_sem=halo_recv.at[1],
        device_id=(chan, win_prev), device_id_type=MESH,
    )

    @pl.when(win < 15)
    def _():
        to_next.start()

    @pl.when(win > 0)
    def _():
        to_prev.start()

    for load in loads:
        load.wait()

    def split(value):
        high = value.astype(jnp.bfloat16)
        return high, (value - high.astype(jnp.float32)).astype(jnp.bfloat16)

    def spectra_of(pieces, q):
        middle = jnp.concatenate(pieces, axis=1)
        high, low = split(jnp.abs(middle))
        total = dot(high, level_ref[...]) + dot(low, level_ref[...])
        normal = middle[:, 128:384] * float(LEVEL) / (total + float(LEVEL * TREND * 1e-05))
        return dot(normal.astype(jnp.bfloat16), table_ref[256 * q : 256 * q + 256, :])

    def inside(h):
        lines = x_ref[pl.ds(h * half, half), :]
        pieces = []
        for p in range(3):
            both = dot(lines[:, 256 * p : 256 * p + 512], trend_ref[...])
            pieces += [both[:, :128], both[:, 128:]]
        return pieces, spectra_of(pieces[0:4], 1) + spectra_of(pieces[2:6], 2)

    def whiten(h, pieces, spectra):
        here = pl.ds(h * half, half)
        first = dot(halo[0, here, :], trend_ref[128:256, :]) + dot(x_ref[here, 0:256], trend_ref[256:512, :])
        last = dot(x_ref[here, 768:1024], trend_ref[0:256, :]) + dot(halo[1, here, :], trend_ref[256:384, :])
        spectra += spectra_of([first] + pieces[0:2], 0) + spectra_of(pieces[4:6] + [last], 3)
        re, im = spectra[:, :NF], spectra[:, NF:]
        size = jnp.sqrt(re * re + im * im)
        high, low = split(size)
        sums = dot(high, smooth_ref[...]) + dot(low, smooth_ref[...])
        level = sums[:, :NF] * (1.0 / SMOOTH) + sums[:, NF:] * (1.0 / NF) + 1e-05
        flags = jnp.broadcast_to(alive_ref[h : h + 1, :], (half, half))
        place = [lax.broadcasted_iota(jnp.int32, (half, half), d) for d in range(2)]
        flags = jnp.where(place[0] == place[1], flags, 0).astype(jnp.float32)
        factor = jnp.sum(flags, axis=1, keepdims=True) / level
        white = jnp.concatenate([re * factor, im * factor], axis=1)
        cbuf[z, h] = white.astype(jnp.bfloat16)

    def ring(p, t, h):
        source = (z + (8 - t, t)[p]) % 8
        return pltpu.make_async_remote_copy(
            src_ref=cbuf.at[source, h], dst_ref=cbuf.at[source, h],
            send_sem=c_send.at[p, t, h], recv_sem=c_recv.at[source, h],
            device_id=(chan, (win_r, win_l)[p]), device_id_type=MESH,
        )

    def ring_arrived(p, t, h):
        source = (z + (8 - t, t)[p]) % 8
        here = cbuf.at[source, h]
        pltpu.make_async_copy(here, here, c_recv.at[source, h]).wait()

    def ring_step(u):
        t = (u + 1) // 2
        for p in range(2):
            h = p if t == 4 else (u + 1) % 2
            ring_arrived(p, t, h)
            if t < 3 or (t == 3 and h == p):
                ring(p, t, h).start()

    def aside(h):
        return pltpu.make_async_remote_copy(
            src_ref=cbuf.at[z, h], dst_ref=moved.at[h],
            send_sem=m_send.at[h], recv_sem=m_recv.at[h],
            device_id=(via_chan[h], win), device_id_type=MESH,
        )

    def swap(source, h):
        return pltpu.make_async_remote_copy(
            src_ref=source, dst_ref=kbuf.at[base + z, h],
            send_sem=s_send.at[h], recv_sem=s_recv.at[h],
            device_id=(swap_chan, swap_win[h]), device_id_type=MESH,
        )

    def held_by(c, h):
        return (c // 8) * 8 + 2 * xor(xor((c // 2) % 4, pair), 2 * h + z0) + c % 2

    def keep(source, h):
        return pltpu.make_async_copy(source, kbuf.at[base + z, h], s_recv.at[h])

    def onward(source, h):
        @pl.when(swaps[h])
        def _():
            swap(source, h).start()

        @pl.when(jnp.logical_not(swaps[h]))
        def _():
            keep(source, h).start()

    def row_other(c):
        return c + 2 - 4 * ((c // 2) % 2)

    def core_other(c):
        return c + 1 - 2 * (c % 2)

    blocks = (
        chan, chan_yo, chan_xp, chan_xm, chan_x2,
        row_other(chan_xp), row_other(chan_xm), row_other(chan_x2),
    )
    targets = (chan_co, chan_xp, chan_xm, chan_x2, chan_yo)

    def spread(b, h, target):
        held = kbuf.at[held_by(blocks[b], h), h]
        return pltpu.make_async_remote_copy(
            src_ref=held, dst_ref=held,
            send_sem=k_send.at[b, h, target], recv_sem=k_recv.at[blocks[b], h],
            device_id=(targets[target], win), device_id_type=MESH,
        )

    def goes_to(b, h):
        if b == 0:
            return ((1, None), (2, None), (4, None), (0, None)) if h == 0 else ((3, None), (1, None), (2, None), (4, None), (0, None))
        if b == 1:
            return ((1, None), (2, None), (3, None), (0, None)) if h == 0 else ((0, None),)
        if b < 5 and h == 1:
            return ((4, None), (0, None))
        if b == 2:
            return ((2, 1), (0, None))
        if b == 3:
            return ((1, 0), (0, None))
        return ((0, None),)

    def spreads(b, h):
        for target, core in goes_to(b, h):
            yield spread(b, h, target), True if core is None else co == core

    def arrived(c, h):
        held = kbuf.at[held_by(c, h), h]
        pltpu.make_async_copy(held, held, k_recv.at[c, h]).wait()

    def pass_on(b, h):
        if b == 0:
            held = kbuf.at[held_by(chan, h), h]
            pltpu.make_async_copy(held, held, s_recv.at[h]).wait()
        else:
            arrived(blocks[b], h)
        for copy, wanted in spreads(b, h):
            if wanted is True:
                copy.start()
            else:
                pl.when(wanted)(copy.start)

    cos, sin = turn_ref[0:1, :], turn_ref[1:2, :]

    def turn(source):
        for h in range(2):
            block = cbuf[source, h].astype(jnp.float32)
            re, im = block[:, :NF], block[:, NF:]
            rc, rs, ic, iss = re * cos, re * sin, im * cos, im * sin
            for lag, (a, b) in enumerate(((rc + iss, ic - rs), (rc - iss, ic + rs))):
                here = pl.ds(lag * rows + h * half, half)
                rot[source, here, :NF] = a.astype(jnp.bfloat16)
                rot[source, here, NF:] = b.astype(jnp.bfloat16)

    def product(which, h):
        total = jnp.zeros((half, LAGS * rows), jnp.float32)
        for seg in range(STEPS):
            total += lax.dot_general(
                kbuf[which * 8 + seg, h], rot[seg], (((1,), (1,)), ((), ())),
                preferred_element_type=jnp.float32,
            )
        return total

    def partial(h):
        return pltpu.make_async_remote_copy(
            src_ref=part_out.at[h], dst_ref=part_in.at[h],
            send_sem=part_send.at[h], recv_sem=part_recv.at[h],
            device_id=(chan, win_other), device_id_type=MESH,
        )

    begun = [inside(h) for h in range(2)]

    @pl.when(win > 0)
    def _():
        to_next.wait_recv()

    @pl.when(win == 0)
    def _():
        halo[0] = jnp.zeros_like(halo[0])

    @pl.when(win < 15)
    def _():
        to_prev.wait_recv()

    @pl.when(win == 15)
    def _():
        halo[1] = jnp.zeros_like(halo[1])

    for h in range(2):
        whiten(h, *begun[h])

        @pl.when(moves[h])
        def _():
            aside(h).start()

        @pl.when(jnp.logical_not(moves[h]))
        def _():
            onward(cbuf.at[z, h], h)

        ring(0, 0, h).start()
        ring(1, 0, h).start()

    for h in range(2):
        @pl.when(moves[h])
        def _():
            aside(h).wait_recv()
            onward(moved.at[h], h)

    turn(z)
    ring_step(1)
    pass_on(0, 1)
    pass_on(0, 0)
    ring_step(2)
    turn((z + 7) % 8)
    turn((z + 1) % 8)
    ring_step(3)
    pass_on(1, 0)
    pass_on(2, 1)
    pass_on(3, 1)
    ring_step(4)
    turn((z + 6) % 8)
    turn((z + 2) % 8)
    pass_on(3, 0)
    pass_on(2, 0)
    pass_on(4, 1)
    ring_step(5)
    ring_step(6)
    turn((z + 5) % 8)
    turn((z + 3) % 8)
    pass_on(1, 1)
    pass_on(4, 0)
    pass_on(5, 0)
    pass_on(6, 0)
    pass_on(7, 0)
    pass_on(5, 1)
    pass_on(6, 1)
    pass_on(7, 1)
    ring_step(7)
    turn((z + 4) % 8)
    def finish(h):
        for b in range(8):
            arrived(core_other(blocks[b]), h)
        part_out[h] = product(1 - yh, h).astype(jnp.bfloat16)
        partial(h).start()

    finish(0)
    finish(1)
    for h in range(2):
        acc[h] = product(yh, h)

    @pl.when(win < 15)
    def _():
        to_next.wait_send()

    @pl.when(win > 0)
    def _():
        to_prev.wait_send()

    for h in range(2):
        @pl.when(swaps[h])
        def _():
            swap(moved.at[h], h).wait_send()

        @pl.when(moves[h])
        def _():
            aside(h).wait_send()

        for p in range(2):
            for t in range(4 if h == p else 3):
                ring(p, t, h).wait_send()
        for b in range(8):
            for copy, wanted in spreads(b, h):
                if wanted is True:
                    copy.wait_send()
                else:
                    pl.when(wanted)(copy.wait_send)
    for h in range(2):
        partial(h).wait_send()
        partial(h).wait_recv()
        out_ref[pl.ds(h * half, half), :] = (acc[h] + part_in[h].astype(jnp.float32)) * scale


def local(strain, alive_flags):
    rows = strain.shape[0]
    half = rows // 2
    scale = 1.0 / math.sqrt(NF * lax.axis_size("win"))
    vmem = pl.BlockSpec(memory_space=pltpu.VMEM)
    tables = constants()
    dma = pltpu.SemaphoreType.DMA
    stacked = pl.pallas_call(
        functools.partial(kernel, scale),
        out_shape=jax.ShapeDtypeStruct((rows, LAGS * rows), jnp.float32),
        in_specs=[pl.BlockSpec(memory_space=pltpu.HBM)] * 7,
        out_specs=vmem,
        scratch_shapes=[
            pltpu.VMEM(strain.shape, jnp.bfloat16),
            pltpu.VMEM((2, half), jnp.int32),
            *(pltpu.VMEM(t.shape, t.dtype) for t in tables),
            dma((7,)),
            pltpu.VMEM((2, rows, 128), jnp.bfloat16),
            pltpu.VMEM((STEPS, 2, half, 2 * NF), jnp.bfloat16),
            pltpu.VMEM((2, half, 2 * NF), jnp.bfloat16),
            pltpu.VMEM((2 * STEPS, 2, half, 2 * NF), jnp.bfloat16),
            pltpu.VMEM((STEPS, LAGS * rows, 2 * NF), jnp.bfloat16),
            pltpu.VMEM((2, half, LAGS * rows), jnp.float32),
            pltpu.VMEM((2, half, LAGS * rows), jnp.bfloat16),
            pltpu.VMEM((2, half, LAGS * rows), jnp.bfloat16),
            dma((2,)), dma((2,)),
            dma((2, 4, 2)), dma((STEPS, 2)),
            dma((2,)), dma((2,)),
            dma((2,)), dma((2,)),
            dma((8, 2, 5)), dma((2 * STEPS, 2)),
            dma((2,)), dma((2,)),
        ],
        compiler_params=pltpu.CompilerParams(
            collective_id=0, has_side_effects=True, vmem_limit_bytes=63 * 1024 * 1024
        ),
        cost_estimate=pl.CostEstimate(
            flops=3_000_000_000, bytes_accessed=4_000_000, transcendentals=0
        ),
    )(strain, alive_flags.reshape(2, half), *tables)
    return stacked.reshape(rows, LAGS, rows)


def solution(mesh):
    return jax.shard_map(
        local,
        mesh=mesh,
        in_specs=(P("chan", "win"), P("chan")),
        out_specs=P("win", None, "chan"),
        check_vma=False,
    )
```

```python
import functools
import math

import jax
import jax.numpy as jnp
import ml_dtypes
import numpy as np
from jax import lax
from jax.experimental import pallas as pl
from jax.experimental.pallas import tpu as pltpu
from jax.sharding import PartitionSpec as P

NF = 256
FIRST_BIN = 64
SEG = 1024
TREND_REACH = 8
LEVEL_REACH = 32
BIN_REACH = 4
LAGS = 2
MESH = pl.DeviceIdType.MESH

TREND = 2 * TREND_REACH + 1
LEVEL = 2 * LEVEL_REACH + 1
SMOOTH = 2 * BIN_REACH + 1
STEPS = 8


def constants():
    bf16 = ml_dtypes.bfloat16
    off = np.arange(512)[:, None] - 128 - np.arange(256)[None, :]
    trend = TREND * (off == 0) - 1.0 * (np.abs(off) <= TREND_REACH)
    level = 1.0 * (np.abs(off) <= LEVEL_REACH)
    k = np.arange(SEG)[:, None]
    f = np.arange(NF)[None, :] + FIRST_BIN
    angle = 2.0 * math.pi / SEG * (k * f % SEG)
    table = np.concatenate([np.cos(angle), -np.sin(angle)], axis=1)
    bins = np.arange(NF)
    near = 1.0 * (np.abs(bins[:, None] - bins[None, :]) <= BIN_REACH)
    smooth = np.concatenate([near, np.ones((NF, NF))], axis=1)
    theta = 2.0 * math.pi / SEG * (f * 2 % SEG)
    turn = np.concatenate([np.cos(theta), np.sin(theta)], axis=0)
    turn = np.concatenate([turn, np.zeros((6, NF))], axis=0)
    return (
        trend.astype(bf16),
        level.astype(bf16),
        table.astype(bf16),
        smooth.astype(bf16),
        turn.astype(np.float32),
    )


def dot(a, b):
    return jnp.dot(a, b, preferred_element_type=jnp.float32)


def kernel(
    scale,
    x_hbm, alive_hbm, trend_hbm, level_hbm, table_hbm, smooth_hbm, turn_hbm,
    out_ref,
    x_ref, alive_ref, trend_ref, level_ref, table_ref, smooth_ref, turn_ref, load_sem,
    halo, cbuf, moved, kbuf, rot, acc, part_out, part_in,
    halo_send, halo_recv, c_send, c_recv, m_send, m_recv, s_send, s_recv, k_send, k_recv, part_send, part_recv,
):
    rows = x_ref.shape[0]
    half = rows // 2
    loads = [
        pltpu.make_async_copy(source, held, load_sem.at[i])
        for i, (source, held) in enumerate((
            (x_hbm, x_ref), (trend_hbm, trend_ref), (level_hbm, level_ref), (table_hbm, table_ref),
            (smooth_hbm, smooth_ref), (alive_hbm, alive_ref), (turn_hbm, turn_ref),
        ))
    ]
    chan = lax.axis_index("chan")
    win = lax.axis_index("win")
    x, yl, co = chan // 4, (chan // 2) % 2, chan % 2
    yh, z = win // 8, win % 8
    z2, z1, z0 = z // 4, (z // 2) % 2, z % 2

    chan_xp = ((x + 1) % 4) * 4 + yl * 2 + co
    chan_xm = ((x + 3) % 4) * 4 + yl * 2 + co
    chan_yo = x * 4 + (1 - yl) * 2 + co
    chan_co = x * 4 + yl * 2 + (1 - co)
    win_r = yh * 8 + (z + 1) % 8
    win_l = yh * 8 + (z + 7) % 8
    win_other = (1 - yh) * 8 + z
    win_next = (win + 1) % 16
    win_prev = (win + 15) % 16

    chan_x2 = ((x + 2) % 4) * 4 + yl * 2 + co
    column, pair = (chan // 2) % 4, z // 2
    base = (chan // 8) * 8

    def xor(a, b):
        return (a // 2 + b // 2) % 2 * 2 + (a + b) % 2

    via = [xor(xor(column, pair), 2 * h + co) for h in range(2)]
    via_chan = [base + 2 * via[h] + co for h in range(2)]
    moves = [via[h] != column for h in range(2)]
    swap_chan = base + 2 * column + z0
    swap_win = [yh * 8 + 2 * via[h] + co for h in range(2)]
    giver_chan = base + 2 * column + z0
    giver_win = [yh * 8 + 2 * xor(xor(column, pair), 2 * h + z0) + co for h in range(2)]
    swaps = [2 * via[h] + co != z for h in range(2)]

    barrier = pltpu.get_barrier_semaphore()
    for device in (
        (chan, win_r), (chan, win_l), (chan, win_next), (chan, win_prev), (chan, win_other),
        (chan_xp, win), (chan_xm, win), (chan_x2, win), (chan_yo, win), (chan_co, win),
    ):
        pl.semaphore_signal(barrier, inc=1, device_id=device, device_id_type=MESH)

    for h in range(2):
        @pl.when(2 * xor(xor(column, pair), 2 * h + z0) + co != z)
        def _():
            pl.semaphore_signal(barrier, inc=1, device_id=(giver_chan, giver_win[h]), device_id_type=MESH)

        @pl.when(moves[h])
        def _():
            pl.semaphore_signal(barrier, inc=1, device_id=(via_chan[h], win), device_id_type=MESH)

    for load in loads:
        load.start()
    pl.semaphore_wait(barrier, 10 + sum(w.astype(jnp.int32) for w in (*swaps, *moves)))

    def to_next(h):
        here = pl.ds(h * half, half)
        return pltpu.make_async_remote_copy(
            src_ref=x_hbm.at[here, SEG - 128 : SEG], dst_ref=halo.at[0, here],
            send_sem=halo_send.at[0, h], recv_sem=halo_recv.at[0, h],
            device_id=(chan, win_next), device_id_type=MESH,
        )

    def to_prev(h):
        here = pl.ds(h * half, half)
        return pltpu.make_async_remote_copy(
            src_ref=x_hbm.at[here, 0:128], dst_ref=halo.at[1, here],
            send_sem=halo_send.at[1, h], recv_sem=halo_recv.at[1, h],
            device_id=(chan, win_prev), device_id_type=MESH,
        )

    for h in range(2):
        @pl.when(win < 15)
        def _():
            to_next(h).start()

        @pl.when(win > 0)
        def _():
            to_prev(h).start()

    for load in loads:
        load.wait()

    def split(value):
        high = value.astype(jnp.bfloat16)
        return high, (value - high.astype(jnp.float32)).astype(jnp.bfloat16)

    def spectra_of(pieces, q):
        middle = jnp.concatenate(pieces, axis=1)
        high, low = split(jnp.abs(middle))
        total = dot(high, level_ref[...]) + dot(low, level_ref[...])
        normal = middle[:, 128:384] * float(LEVEL) / (total + float(LEVEL * TREND * 1e-05))
        return dot(normal.astype(jnp.bfloat16), table_ref[256 * q : 256 * q + 256, :])

    def inside(h):
        lines = x_ref[pl.ds(h * half, half), :]
        pieces = []
        for p in range(3):
            both = dot(lines[:, 256 * p : 256 * p + 512], trend_ref[...])
            pieces += [both[:, :128], both[:, 128:]]
        return pieces, spectra_of(pieces[0:4], 1) + spectra_of(pieces[2:6], 2)

    def whiten(h, pieces, spectra):
        here = pl.ds(h * half, half)
        first = dot(halo[0, here, :], trend_ref[128:256, :]) + dot(x_ref[here, 0:256], trend_ref[256:512, :])
        last = dot(x_ref[here, 768:1024], trend_ref[0:256, :]) + dot(halo[1, here, :], trend_ref[256:384, :])
        spectra += spectra_of([first] + pieces[0:2], 0) + spectra_of(pieces[4:6] + [last], 3)
        re, im = spectra[:, :NF], spectra[:, NF:]
        size = jnp.sqrt(re * re + im * im)
        high, low = split(size)
        sums = dot(high, smooth_ref[...]) + dot(low, smooth_ref[...])
        level = sums[:, :NF] * (1.0 / SMOOTH) + sums[:, NF:] * (1.0 / NF) + 1e-05
        flags = jnp.broadcast_to(alive_ref[h : h + 1, :], (half, half))
        place = [lax.broadcasted_iota(jnp.int32, (half, half), d) for d in range(2)]
        flags = jnp.where(place[0] == place[1], flags, 0).astype(jnp.float32)
        factor = jnp.sum(flags, axis=1, keepdims=True) / level
        white = jnp.concatenate([re * factor, im * factor], axis=1)
        cbuf[z, h] = white.astype(jnp.bfloat16)

    def ring(p, t, h):
        source = (z + (8 - t, t)[p]) % 8
        return pltpu.make_async_remote_copy(
            src_ref=cbuf.at[source, h], dst_ref=cbuf.at[source, h],
            send_sem=c_send.at[p, t, h], recv_sem=c_recv.at[source, h],
            device_id=(chan, (win_r, win_l)[p]), device_id_type=MESH,
        )

    def ring_arrived(p, t, h):
        source = (z + (8 - t, t)[p]) % 8
        here = cbuf.at[source, h]
        pltpu.make_async_copy(here, here, c_recv.at[source, h]).wait()

    def ring_step(u):
        t = (u + 1) // 2
        for p in range(2):
            h = p if t == 4 else (u + 1) % 2
            ring_arrived(p, t, h)
            if t < 3 or (t == 3 and h == p):
                ring(p, t, h).start()

    def aside(h):
        return pltpu.make_async_remote_copy(
            src_ref=cbuf.at[z, h], dst_ref=moved.at[h],
            send_sem=m_send.at[h], recv_sem=m_recv.at[h],
            device_id=(via_chan[h], win), device_id_type=MESH,
        )

    def swap(source, h):
        return pltpu.make_async_remote_copy(
            src_ref=source, dst_ref=kbuf.at[base + z, h],
            send_sem=s_send.at[h], recv_sem=s_recv.at[h],
            device_id=(swap_chan, swap_win[h]), device_id_type=MESH,
        )

    def held_by(c, h):
        return (c // 8) * 8 + 2 * xor(xor((c // 2) % 4, pair), 2 * h + z0) + c % 2

    def keep(source, h):
        return pltpu.make_async_copy(source, kbuf.at[base + z, h], s_recv.at[h])

    def onward(source, h):
        @pl.when(swaps[h])
        def _():
            swap(source, h).start()

        @pl.when(jnp.logical_not(swaps[h]))
        def _():
            keep(source, h).start()

    def row_other(c):
        return c + 2 - 4 * ((c // 2) % 2)

    def core_other(c):
        return c + 1 - 2 * (c % 2)

    blocks = (
        chan, chan_yo, chan_xp, chan_xm, chan_x2,
        row_other(chan_xp), row_other(chan_xm), row_other(chan_x2),
    )
    targets = (chan_co, chan_xp, chan_xm, chan_x2, chan_yo)

    def spread(b, h, target):
        held = kbuf.at[held_by(blocks[b], h), h]
        return pltpu.make_async_remote_copy(
            src_ref=held, dst_ref=held,
            send_sem=k_send.at[b, h, target], recv_sem=k_recv.at[blocks[b], h],
            device_id=(targets[target], win), device_id_type=MESH,
        )

    def goes_to(b, h):
        if b == 0:
            return ((1, None), (2, None), (4, None), (0, None)) if h == 0 else ((3, None), (1, None), (2, None), (4, None), (0, None))
        if b == 1:
            return ((1, None), (2, None), (3, None), (0, None)) if h == 0 else ((0, None),)
        if b < 5 and h == 1:
            return ((4, None), (0, None))
        if b == 2:
            return ((2, 1), (0, None))
        if b == 3:
            return ((1, 0), (0, None))
        return ((0, None),)

    def spreads(b, h):
        for target, core in goes_to(b, h):
            yield spread(b, h, target), True if core is None else co == core

    def arrived(c, h):
        held = kbuf.at[held_by(c, h), h]
        pltpu.make_async_copy(held, held, k_recv.at[c, h]).wait()

    def pass_on(b, h):
        if b == 0:
            held = kbuf.at[held_by(chan, h), h]
            pltpu.make_async_copy(held, held, s_recv.at[h]).wait()
        else:
            arrived(blocks[b], h)
        for copy, wanted in spreads(b, h):
            if wanted is True:
                copy.start()
            else:
                pl.when(wanted)(copy.start)

    cos, sin = turn_ref[0:1, :], turn_ref[1:2, :]

    def turn(source):
        for h in range(2):
            block = cbuf[source, h].astype(jnp.float32)
            re, im = block[:, :NF], block[:, NF:]
            rc, rs, ic, iss = re * cos, re * sin, im * cos, im * sin
            for lag, (a, b) in enumerate(((rc + iss, ic - rs), (rc - iss, ic + rs))):
                here = pl.ds(lag * rows + h * half, half)
                rot[source, here, :NF] = a.astype(jnp.bfloat16)
                rot[source, here, NF:] = b.astype(jnp.bfloat16)

    def product(which, h):
        total = jnp.zeros((half, LAGS * rows), jnp.float32)
        for seg in range(STEPS):
            total += lax.dot_general(
                kbuf[which * 8 + seg, h], rot[seg], (((1,), (1,)), ((), ())),
                preferred_element_type=jnp.float32,
            )
        return total

    def partial(h):
        return pltpu.make_async_remote_copy(
            src_ref=part_out.at[h], dst_ref=part_in.at[h],
            send_sem=part_send.at[h], recv_sem=part_recv.at[h],
            device_id=(chan, win_other), device_id_type=MESH,
        )

    begun = [inside(h) for h in range(2)]

    @pl.when(win == 0)
    def _():
        halo[0] = jnp.zeros_like(halo[0])

    @pl.when(win == 15)
    def _():
        halo[1] = jnp.zeros_like(halo[1])

    for h in range(2):
        @pl.when(win > 0)
        def _():
            to_next(h).wait_recv()

        @pl.when(win < 15)
        def _():
            to_prev(h).wait_recv()

        whiten(h, *begun[h])

        ring(0, 0, h).start()
        ring(1, 0, h).start()

        @pl.when(moves[h])
        def _():
            aside(h).start()

        @pl.when(jnp.logical_not(moves[h]))
        def _():
            onward(cbuf.at[z, h], h)


    for h in range(2):
        @pl.when(moves[h])
        def _():
            aside(h).wait_recv()
            onward(moved.at[h], h)

    turn(z)
    ring_step(1)
    pass_on(0, 1)
    pass_on(0, 0)
    ring_step(2)
    turn((z + 7) % 8)
    turn((z + 1) % 8)
    ring_step(3)
    pass_on(1, 0)
    pass_on(2, 1)
    pass_on(3, 1)
    ring_step(4)
    turn((z + 6) % 8)
    turn((z + 2) % 8)
    pass_on(3, 0)
    pass_on(2, 0)
    pass_on(4, 1)
    ring_step(5)
    ring_step(6)
    turn((z + 5) % 8)
    turn((z + 3) % 8)
    pass_on(1, 1)
    pass_on(4, 0)
    pass_on(5, 0)
    pass_on(6, 0)
    pass_on(7, 0)
    pass_on(5, 1)
    pass_on(6, 1)
    pass_on(7, 1)
    ring_step(7)
    turn((z + 4) % 8)
    def finish(h):
        for b in range(8):
            arrived(core_other(blocks[b]), h)
        part_out[h] = product(1 - yh, h).astype(jnp.bfloat16)
        partial(h).start()

    finish(0)
    finish(1)
    for h in range(2):
        acc[h] = product(yh, h)

    for h in range(2):
        @pl.when(win < 15)
        def _():
            to_next(h).wait_send()

        @pl.when(win > 0)
        def _():
            to_prev(h).wait_send()

    for h in range(2):
        @pl.when(swaps[h])
        def _():
            swap(moved.at[h], h).wait_send()

        @pl.when(moves[h])
        def _():
            aside(h).wait_send()

        for p in range(2):
            for t in range(4 if h == p else 3):
                ring(p, t, h).wait_send()
        for b in range(8):
            for copy, wanted in spreads(b, h):
                if wanted is True:
                    copy.wait_send()
                else:
                    pl.when(wanted)(copy.wait_send)
    for h in range(2):
        partial(h).wait_send()
        partial(h).wait_recv()
        out_ref[pl.ds(h * half, half), :] = (acc[h] + part_in[h].astype(jnp.float32)) * scale


def local(strain, alive_flags):
    rows = strain.shape[0]
    half = rows // 2
    scale = 1.0 / math.sqrt(NF * lax.axis_size("win"))
    vmem = pl.BlockSpec(memory_space=pltpu.VMEM)
    tables = constants()
    dma = pltpu.SemaphoreType.DMA
    stacked = pl.pallas_call(
        functools.partial(kernel, scale),
        out_shape=jax.ShapeDtypeStruct((rows, LAGS * rows), jnp.float32),
        in_specs=[pl.BlockSpec(memory_space=pltpu.HBM)] * 7,
        out_specs=vmem,
        scratch_shapes=[
            pltpu.VMEM(strain.shape, jnp.bfloat16),
            pltpu.VMEM((2, half), jnp.int32),
            *(pltpu.VMEM(t.shape, t.dtype) for t in tables),
            dma((7,)),
            pltpu.VMEM((2, rows, 128), jnp.bfloat16),
            pltpu.VMEM((STEPS, 2, half, 2 * NF), jnp.bfloat16),
            pltpu.VMEM((2, half, 2 * NF), jnp.bfloat16),
            pltpu.VMEM((2 * STEPS, 2, half, 2 * NF), jnp.bfloat16),
            pltpu.VMEM((STEPS, LAGS * rows, 2 * NF), jnp.bfloat16),
            pltpu.VMEM((2, half, LAGS * rows), jnp.float32),
            pltpu.VMEM((2, half, LAGS * rows), jnp.bfloat16),
            pltpu.VMEM((2, half, LAGS * rows), jnp.bfloat16),
            dma((2, 2)), dma((2, 2)),
            dma((2, 4, 2)), dma((STEPS, 2)),
            dma((2,)), dma((2,)),
            dma((2,)), dma((2,)),
            dma((8, 2, 5)), dma((2 * STEPS, 2)),
            dma((2,)), dma((2,)),
        ],
        compiler_params=pltpu.CompilerParams(
            collective_id=0, has_side_effects=True, vmem_limit_bytes=63 * 1024 * 1024
        ),
        cost_estimate=pl.CostEstimate(
            flops=3_000_000_000, bytes_accessed=4_000_000, transcendentals=0
        ),
    )(strain, alive_flags.reshape(2, half), *tables)
    return stacked.reshape(rows, LAGS, rows)


def solution(mesh):
    return jax.shard_map(
        local,
        mesh=mesh,
        in_specs=(P("chan", "win"), P("chan")),
        out_specs=P("win", None, "chan"),
        check_vma=False,
    )
```
